32 devices in a mesh: ctx: 8 (over z, y), head: 4 (over x, core).
Axes of the slice: x: 2, y: 2, z: 4, core: 2. Of those that a mesh axis runs over, the one named last changes fastest.
Arguments:
- query_nope: bfloat16 [2048, 8192], P('ctx', 'head'), may hold values from -6 to 6
- query_rope: bfloat16 [2048, 4096], P('ctx', 'head'), may hold values from -8 to 8
- latent_cache: bfloat16 [2048, 512], P('ctx'), may hold values from -6 to 6
- key_rope: bfloat16 [2048, 64], P('ctx'), may hold values from -8 to 8
- key_up: bfloat16 [64, 128, 512], P('head'), may hold values from -0.5 to 0.5
- value_up: bfloat16 [64, 512, 128], P('head'), may hold values from -0.25 to 0.25
- out_proj: bfloat16 [8192, 7168], P('head', 'ctx'), may hold values from -0.0625 to 0.0625
- group_order: int32 [16], replicated, may hold values from 0 to 15, each once
Outputs:
- attended: bfloat16 [2048, 7168], P(('ctx', 'head'))
The draws below stay inside these ranges and needn't reach their ends.
Inputs may be any that keep to these rules, and one draw needn't show every extreme that they name: `group_order`: entry j names the document group stored at rows j * 128 onward; each group appears once.
All inputs are finite; a program needn't handle non-finite values.
Results may differ from the reference program's by a relative error of at most 0.012.
Values may be sent and summed in bfloat16 or wider, within the bound.
No kernel may reach another device: no remote copies, remote signals or barrier semaphores. Data moves between devices by JAX's collectives and lax.ppermute only.
A program may use at most 192 MiB of HBM per device.

```python
import jax
import jax.numpy as jnp
from jax import lax

HEADS = 64
LATENT = 512
ROPE = 64
NOPE = 128
VDIM = 128
D = 7168
GROUP = 128
GROUPS = 16
TOKENS = 2048


def draw_key_rope(key, part):
    key = jax.random.fold_in(key, 21)
    values = jnp.clip(jax.random.normal(key, (TOKENS, ROPE), jnp.float32), -6.0, 6.0)
    return values.astype(jnp.bfloat16)


def draw_query_rope(key, part):
    key = jax.random.fold_in(key, 22)
    values = jnp.clip(jax.random.normal(key, (TOKENS, HEADS * ROPE), jnp.float32), -6.0, 6.0)
    return values.astype(jnp.bfloat16)


def shard_levels(rng, dims, split, low, high):
    def one(dim, parts):
        heights = jax.random.uniform(jax.random.fold_in(jax.random.fold_in(rng, 6), dim), (parts,), jnp.float32, low / len(split), high / len(split))
        return jnp.repeat(jnp.exp(heights), dims[dim] // parts).reshape((-1,) + (1,) * (len(dims) - dim - 1))

    loudness = one(*split[0])
    for cut in split[1:]:
        loudness = loudness * one(*cut)
    return loudness


def gaussian(stream_key, dims, width, limit, shards=(), kind=jnp.bfloat16):
    gain = shard_levels(stream_key, dims, shards, -0.22, 0.18) if shards else 1.0
    values = jax.random.normal(stream_key, dims, jnp.float32) * width * gain
    return jnp.minimum(jnp.maximum(values, -limit), limit).astype(kind)


def setup_inputs(seed: int = 0) -> dict:
    key_list = jax.random.split(jax.random.key(seed), 9)
    query_nope = gaussian(key_list[0], (TOKENS, HEADS * NOPE), 1.0, 6.0, ((0, 8), (1, 4)))
    query_rope = draw_query_rope(jax.random.fold_in(key_list[8], 71), 0)
    latent_cache = gaussian(key_list[2], (TOKENS, LATENT), 1.0, 6.0, ((0, 8),))
    key_rope = draw_key_rope(jax.random.fold_in(key_list[8], 71), 0)
    key_up = gaussian(key_list[4], (HEADS, NOPE, LATENT), NOPE ** -0.5, 0.5, ((0, 4),))
    value_up = gaussian(key_list[5], (HEADS, LATENT, VDIM), LATENT ** -0.5, 0.25, ((0, 4),))
    out_proj = gaussian(key_list[6], (HEADS * VDIM, D), (HEADS * VDIM) ** -0.5, 0.0625, ((0, 4), (1, 8)))
    group_order = jax.random.permutation(key_list[7], GROUPS).astype(jnp.int32)
    return dict(query_nope=query_nope, query_rope=query_rope, latent_cache=latent_cache, key_rope=key_rope, key_up=key_up, value_up=value_up, out_proj=out_proj, group_order=group_order)


def reference(query_nope, query_rope, latent_cache, key_rope, key_up, value_up, out_proj, group_order):
    scale = (NOPE + ROPE) ** -0.5
    stored = jnp.arange(TOKENS, dtype=jnp.int32)
    position = group_order[stored // GROUP] * GROUP + stored % GROUP
    visible = position[None, :] <= position[:, None]
    nope_parts = query_nope.reshape(TOKENS, HEADS, NOPE)
    rope_parts = query_rope.reshape(TOKENS, HEADS, ROPE)

    def one_head(head):
        absorbed = jnp.dot(nope_parts[:, head], key_up[head], preferred_element_type=jnp.float32).astype(jnp.bfloat16)
        scores = jnp.dot(absorbed, latent_cache.T, preferred_element_type=jnp.float32)
        scores = scores + jnp.dot(rope_parts[:, head], key_rope.T, preferred_element_type=jnp.float32)
        scores = jnp.where(visible, scores * scale, -jnp.inf)
        weights = jnp.exp(scores - jnp.max(scores, axis=1, keepdims=True))
        total = jnp.sum(weights, axis=1)
        mixed = jnp.dot(weights.astype(jnp.bfloat16), latent_cache, preferred_element_type=jnp.float32)
        latent_out = (mixed / total[:, None]).astype(jnp.bfloat16)
        return jnp.dot(latent_out, value_up[head], preferred_element_type=jnp.float32).astype(jnp.bfloat16)

    head_out = lax.map(one_head, jnp.arange(HEADS, dtype=jnp.int32))
    head_out = jnp.transpose(head_out, (1, 0, 2)).reshape(TOKENS, HEADS * VDIM)
    return jnp.dot(head_out, out_proj, preferred_element_type=jnp.float32).astype(jnp.bfloat16)
```

```python
import functools

import jax
import jax.numpy as jnp
from jax import lax
from jax.experimental import pallas as pl
from jax.experimental.pallas import tpu as pltpu
from jax.sharding import PartitionSpec as P

LATENT = 512
ROPE = 64
NOPE = 128
VDIM = 128
GROUP = 128
PAIR = 2
STEP_ROWS = 16
PAD = 128
VMEM = 40 * 1024 * 1024
SMALL_VMEM = 24 * 1024 * 1024
LIGHT = pl.CostEstimate(flops=1, bytes_accessed=1, transcendentals=0)


def ring_offsets(layers):
    offsets = [0]
    for step in range(1, layers // 2 + 1):
        offsets.append(step)
        if step < layers - step:
            offsets.append(-step)
    return offsets


def ring_pairs(layers, shift):
    return [
        (z * PAIR + y, (z + shift) % layers * PAIR + y) for z in range(layers) for y in range(PAIR)
    ]


def swap_pairs(size, bit):
    return [(i, i ^ bit) for i in range(size)]


def ring_gather(block, layers):
    blocks = {0: block}
    for offset in ring_offsets(layers)[1:]:
        step = 1 if offset > 0 else -1
        blocks[offset] = lax.ppermute(blocks[offset - step], "ctx", ring_pairs(layers, step))
    return [blocks[offset] for offset in ring_offsets(layers)]


def bit_reversed(index, size):
    out = 0
    while size > 1:
        out, index, size = out * 2 + index % 2, index // 2, size // 2
    return out


def prepare_kernel(offsets, scalars, order, latent_ref, rope_ref, packed_ref, key_pos_ref, query_pos_ref):
    me, y, z = scalars[1], scalars[2], scalars[3]
    block_rows = packed_ref.shape[0]
    chunks, rows, lanes = query_pos_ref.shape
    tok_rows = latent_ref.shape[0]
    layers, half = len(offsets), key_pos_ref.shape[1] // (PAIR * block_rows)
    first = pl.multiple_of(me * block_rows, block_rows)
    packed_ref[:, :LATENT] = latent_ref[pl.ds(first, block_rows), :]
    packed_ref[:, LATENT:] = jnp.concatenate(
        [rope_ref[pl.ds(first, block_rows), :], jnp.zeros((block_rows, PAD - ROPE), jnp.bfloat16)], 1
    )

    def position(row):
        group, out = row // GROUP, jnp.zeros_like(row)
        for g in range(order.shape[0]):
            out = jnp.where(group == g, order[g], out)
        return out * GROUP + row % GROUP

    shape = key_pos_ref.shape
    piece = lax.broadcasted_iota(jnp.int32, shape, 0)
    lane = lax.broadcasted_iota(jnp.int32, shape, 1)
    offset = jnp.zeros(shape, jnp.int32)
    for place, o in enumerate(offsets):
        offset = jnp.where(piece // 2 == place, o, offset)
    block = lane // (PAIR * block_rows)
    head = bit_reversed(block, half) * 2 + piece % 2 if half > 1 else piece % 2
    ctx = (z - offset + layers) % layers * PAIR + (y ^ (lane // block_rows % PAIR))
    key_pos_ref[...] = position(ctx * tok_rows + (head ^ me) * block_rows + lane % block_rows)

    shape = (rows, lanes)
    row = lax.broadcasted_iota(jnp.int32, shape, 0)
    base = (z * PAIR + y) * tok_rows + (row // STEP_ROWS ^ me) * block_rows + row % STEP_ROWS
    for chunk in range(chunks):
        query_pos_ref[chunk] = position(base + chunk * STEP_ROWS)


def prepare(scalars, order, latent, rope, blocks, offsets):
    tok_rows = latent.shape[0]
    block_rows = tok_rows // blocks
    chunks = block_rows // STEP_ROWS
    pieces, keys = 2 * len(offsets), PAIR * block_rows * blocks // 2
    vmem, smem = pl.BlockSpec(memory_space=pltpu.VMEM), pl.BlockSpec(memory_space=pltpu.SMEM)
    return pl.pallas_call(
        functools.partial(prepare_kernel, offsets),
        in_specs=[smem, smem, vmem, vmem],
        out_specs=[vmem, vmem, vmem],
        out_shape=[
            jax.ShapeDtypeStruct((block_rows, LATENT + PAD), jnp.bfloat16),
            jax.ShapeDtypeStruct((pieces, keys), jnp.int32),
            jax.ShapeDtypeStruct((chunks, blocks * STEP_ROWS, 128), jnp.int32),
        ],
        cost_estimate=LIGHT,
        name="prepare",
    )(scalars, order, latent, rope)


def absorb_kernel(scalars, nope_ref, rope_ref, key_up_ref, query_ref, rotary_ref):
    chunks, heads, rows, _ = query_ref.shape
    blocks = rows // STEP_ROWS
    me = scalars[1]
    for head in range(heads):
        nope = jnp.concatenate(
            [
                nope_ref[b ^ me, c, :, head * NOPE : (head + 1) * NOPE]
                for c in range(chunks)
                for b in range(blocks)
            ],
            0,
        )
        absorbed = jnp.dot(nope, key_up_ref[head], preferred_element_type=jnp.float32)
        absorbed = absorbed.astype(jnp.bfloat16)
        for c in range(chunks):
            query_ref[c, head] = absorbed[c * rows : (c + 1) * rows]
            rotary_ref[c, head] = jnp.concatenate(
                [rope_ref[b ^ me, c, :, head * ROPE : (head + 1) * ROPE] for b in range(blocks)], 0
            )


def absorb(scalars, nope, rope, key_up):
    blocks, chunks, step_rows, _ = nope.shape
    heads, rows = key_up.shape[0], blocks * step_rows
    group = min(4, heads)
    spec = pl.BlockSpec
    return pl.pallas_call(
        absorb_kernel,
        grid_spec=pltpu.PrefetchScalarGridSpec(
            num_scalar_prefetch=1,
            grid=(heads // group,),
            in_specs=[
                spec((blocks, chunks, step_rows, group * NOPE), lambda i, s: (0, 0, 0, i)),
                spec((blocks, chunks, step_rows, group * ROPE), lambda i, s: (0, 0, 0, i)),
                spec((group, NOPE, LATENT), lambda i, s: (i, 0, 0)),
            ],
            out_specs=[
                spec((chunks, group, rows, LATENT), lambda i, s: (0, i, 0, 0)),
                spec((chunks, group, rows, ROPE), lambda i, s: (0, i, 0, 0)),
            ],
        ),
        out_shape=[
            jax.ShapeDtypeStruct((chunks, heads, rows, LATENT), jnp.bfloat16),
            jax.ShapeDtypeStruct((chunks, heads, rows, ROPE), jnp.bfloat16),
        ],
        compiler_params=pltpu.CompilerParams(vmem_limit_bytes=SMALL_VMEM),
        cost_estimate=LIGHT,
        name="absorb",
    )(scalars, nope, rope, key_up)


def attention_kernel(scalars, query_ref, rotary_ref, value_up_ref, query_pos_ref, key_pos_ref, *refs):
    piece_refs, out_ref = refs[:-1], refs[-1]
    heads, rows = query_ref.shape[1], query_ref.shape[2]
    scale = (NOPE + ROPE) ** (-0.5)
    query = query_ref[...].reshape(heads * rows, LATENT)
    rotary = rotary_ref[...].reshape(heads * rows, ROPE)
    query_pos = jnp.concatenate([query_pos_ref[0, :, :1]] * heads, 0)
    contract = (((1,), (1,)), ((), ()))
    steps = len(piece_refs) // 2

    def latent(step):
        return jnp.concatenate([ref[:, :LATENT] for ref in piece_refs[2 * step : 2 * step + 2]], 0)

    def products(step):
        keys = jnp.concatenate(
            [ref[:, LATENT : LATENT + ROPE] for ref in piece_refs[2 * step : 2 * step + 2]], 0
        )
        out = lax.dot_general(query, latent(step), contract, preferred_element_type=jnp.float32)
        return out + lax.dot_general(rotary, keys, contract, preferred_element_type=jnp.float32)

    top = jnp.full((heads * rows, 1), -1e30, jnp.float32)
    total = jnp.zeros((heads * rows, 1), jnp.float32)
    mixed = jnp.zeros((heads * rows, LATENT), jnp.float32)
    scores = products(0)
    for step in range(steps):
        later = products(step + 1) if step + 1 < steps else None
        key_pos = jnp.concatenate([key_pos_ref[2 * step + i : 2 * step + i + 1] for i in range(2)], 1)
        scores = jnp.where(key_pos <= query_pos, scores, -jnp.inf)
        new_top = jnp.maximum(top, jnp.max(scores, axis=1, keepdims=True))
        fade = jnp.exp((top - new_top) * scale)
        weights = jnp.exp((scores - new_top) * scale)
        total = total * fade + jnp.sum(weights, axis=1, keepdims=True)
        mixed = mixed * fade + jnp.dot(
            weights.astype(jnp.bfloat16), latent(step), preferred_element_type=jnp.float32
        )
        top, scores = new_top, later
    mixed = (mixed / total).astype(jnp.bfloat16)
    for head in range(heads):
        out_ref[:, head * VDIM : (head + 1) * VDIM] = jnp.dot(
            mixed[head * rows : (head + 1) * rows],
            value_up_ref[head],
            preferred_element_type=jnp.float32,
        ).astype(jnp.bfloat16)


def attend(scalars, query, rotary, value_up, query_pos, key_pos, pieces, chunk):
    _, heads, rows, _ = query.shape
    heads //= PAIR
    keys = key_pos.size
    spec = pl.BlockSpec
    return pl.pallas_call(
        attention_kernel,
        grid_spec=pltpu.PrefetchScalarGridSpec(
            num_scalar_prefetch=1,
            grid=(1,),
            in_specs=[
                spec((1, heads, rows, LATENT), lambda i, s: (chunk, s[0], 0, 0)),
                spec((1, heads, rows, ROPE), lambda i, s: (chunk, s[0], 0, 0)),
                spec((heads, LATENT, VDIM), lambda i, s: (s[0], 0, 0)),
                spec((1, rows, 128), lambda i, s: (chunk, 0, 0)),
                spec(key_pos.shape, lambda i, s: (0, 0)),
            ]
            + [spec(piece.shape, lambda i, s: (0, 0)) for piece in pieces],
            out_specs=spec((rows, heads * VDIM), lambda i, s: (0, 0)),
        ),
        out_shape=jax.ShapeDtypeStruct((rows, heads * VDIM), jnp.bfloat16),
        compiler_params=pltpu.CompilerParams(vmem_limit_bytes=VMEM),
        cost_estimate=LIGHT,
        name="attention",
    )(scalars, query, rotary, value_up, query_pos, key_pos, *pieces)


def projection_kernel(layers, blocks, scalars, *refs):
    pieces, (mine_ref, *other_refs), (keep_ref, send_ref) = refs[:layers], refs[layers:-2], refs[-2:]
    left = jnp.concatenate([piece[...] for piece in pieces], 0)

    def product(*right_refs):
        right = jnp.concatenate([ref[...] for ref in right_refs], 0)
        out = jnp.dot(left, right, preferred_element_type=jnp.float32).astype(jnp.bfloat16)
        for layer in range(layers):
            for y in range(PAIR):
                for block in range(blocks):
                    first = ((layer * PAIR + y) * blocks + block) * STEP_ROWS
                    place = bit_reversed(block, blocks)
                    ref = keep_ref if place < blocks // 2 else send_ref
                    ref[place % (blocks // 2), y, layer, 0] = out[first : first + STEP_ROWS]

    @pl.when(pl.program_id(0) == 0)
    def _():
        product(mine_ref)

    @pl.when(pl.program_id(0) == 1)
    def _():
        product(*other_refs)


def project(scalars, pieces, mine, others, blocks):
    layers = len(pieces)
    depth, columns = mine.shape
    rows = pieces[0].shape[0]
    spec = pl.BlockSpec
    shape = (blocks // 2, PAIR, layers)
    out_spec = spec((*shape, 1, STEP_ROWS, columns), lambda i, s: (0, 0, 0, s[2] ^ i, 0, 0))
    out_shape = jax.ShapeDtypeStruct((*shape, PAIR, STEP_ROWS, columns), jnp.bfloat16)
    return pl.pallas_call(
        functools.partial(projection_kernel, layers, blocks),
        grid_spec=pltpu.PrefetchScalarGridSpec(
            num_scalar_prefetch=1,
            grid=(PAIR,),
            in_specs=[spec((rows, depth), lambda i, s: (0, 0))] * layers
            + [spec(right.shape, lambda i, s: (0, 0)) for right in (mine, *others)],
            out_specs=[out_spec, out_spec],
        ),
        out_shape=[out_shape, out_shape],
        compiler_params=pltpu.CompilerParams(vmem_limit_bytes=SMALL_VMEM),
        cost_estimate=LIGHT,
        name="projection",
    )(scalars, *pieces, mine, *others)


def add(a, b):
    return (a.astype(jnp.float32) + b.astype(jnp.float32)).astype(jnp.bfloat16)


def after(value, *others):
    return lax.optimization_barrier((value, others))[0]


def assemble_kernel(offsets, scalars, *refs):
    refs, out_ref = refs[:-1], refs[-1]
    layers = len(offsets)
    columns = refs[0].shape[-1]
    z = scalars[3]
    for index, ref in enumerate(refs):
        chunk, offset = index // layers, offsets[index % layers]
        layer = (z + offset + layers) % layers
        for y in range(PAIR):
            first = pl.multiple_of((layer * PAIR + y) * columns, columns)
            rows = slice(chunk * STEP_ROWS, (chunk + 1) * STEP_ROWS)
            out_ref[rows, pl.ds(first, columns)] = ref[y]


def assemble(scalars, outs, offsets, z):
    chunks, layers = len(outs), len(offsets)
    columns = outs[0][0].shape[-1]
    if columns % 128:
        rows = []
        for chunk in range(chunks):
            arrived = dict(zip([offset % layers for offset in offsets], outs[chunk]))
            row = jnp.stack([arrived[offset] for offset in range(layers)], 0)
            row = jnp.transpose(jnp.roll(row, z, axis=0), (2, 0, 1, 3))
            rows.append(row.reshape(STEP_ROWS, -1))
        return jnp.concatenate(rows, 0)
    vmem, smem = pl.BlockSpec(memory_space=pltpu.VMEM), pl.BlockSpec(memory_space=pltpu.SMEM)
    return pl.pallas_call(
        functools.partial(assemble_kernel, offsets),
        in_specs=[smem] + [vmem] * (chunks * layers),
        out_specs=vmem,
        out_shape=jax.ShapeDtypeStruct(
            (chunks * STEP_ROWS, layers * PAIR * columns), outs[0][0].dtype
        ),
        cost_estimate=LIGHT,
        name="assemble",
    )(scalars, *[block for chunk in range(chunks) for block in outs[chunk]])


def per_device(
    devices, blocks, query_nope, query_rope, latent_cache, key_rope, key_up, value_up, out_proj,
    group_order,
):
    layers = devices // PAIR
    offsets = ring_offsets(layers)
    chunks = query_nope.shape[0] // blocks // STEP_ROWS
    depth = out_proj.shape[0] // PAIR
    ctx, me = lax.axis_index("ctx"), lax.axis_index("head")
    z, y = ctx // PAIR, ctx % PAIR
    pair = swap_pairs(devices, 1)
    scalars_keep = jnp.stack([y, me, y, z]).astype(jnp.int32)
    scalars_send = jnp.stack([1 - y, me, y, z]).astype(jnp.int32)

    nope = query_nope.reshape(blocks, chunks, STEP_ROWS, -1)
    rope = query_rope.reshape(blocks, chunks, STEP_ROWS, -1)

    packed, key_pos, query_pos = prepare(
        scalars_keep, group_order, latent_cache, key_rope, blocks, offsets
    )
    packed = jnp.concatenate([packed, lax.ppermute(packed, "ctx", pair)], 0)
    mine = lax.dynamic_slice_in_dim(out_proj, y * depth, depth, 0)
    other = lax.dynamic_slice_in_dim(out_proj, (1 - y) * depth, depth, 0)
    query, rotary = absorb(after(scalars_keep, packed), nope, rope, key_up)
    cuts = [0, depth * 3 // 8, depth * 6 // 8, depth]
    others = []
    for first, end in zip(cuts[:-1], cuts[1:]):
        if others:
            other = after(other, others[-1])
        others.append(lax.ppermute(after(other[first:end], packed), "ctx", pair))
    pieces = ring_gather(packed, layers)
    pieces[1] = after(pieces[1], query, mine)
    keys = []
    for piece in pieces:
        bit = blocks // 2
        while bit > 1:
            piece = jnp.concatenate(
                [piece, lax.ppermute(piece, "head", swap_pairs(blocks, bit))], 0
            )
            bit //= 2
        keys += [piece, lax.ppermute(piece, "head", swap_pairs(blocks, 1))]

    last = others[1]
    gathered, sums, outs = {}, {}, {}

    def attention_stage(chunk, *arrived):
        nonlocal last
        args = [value_up, query_pos, key_pos, keys, chunk]
        sent = attend(scalars_send, after(query, last, arrived), rotary, *args)
        swapped = lax.ppermute(sent, "ctx", pair)
        last = kept = attend(scalars_keep, after(query, sent), rotary, *args)
        gathered[chunk] = {0: jnp.concatenate([kept, swapped], 0)}

    def ring_stage(chunk, offset):
        held = gathered[chunk]
        step = 1 if offset > 0 else -1
        held[offset] = lax.ppermute(held[offset - step], "ctx", ring_pairs(layers, step))

    def projection_stage(chunk):
        nonlocal last
        pieces = [gathered[chunk][offset] for offset in offsets]
        pieces[0] = after(pieces[0], last)
        sums[chunk] = project(scalars_keep, pieces, mine, others, blocks)
        last = sums[chunk][0]

    def head_stage(chunk, bit):
        nonlocal last
        keep, send = sums[chunk]
        got = after(lax.ppermute(send, "head", swap_pairs(blocks, bit)), last)
        left = keep.shape[0] // 2
        if left:
            sums[chunk] = add(keep[:left], got[:left]), add(keep[left:], got[left:])
        else:
            sums[chunk] = add(keep[0, 0], got[0, 0]), add(keep[0, 1], got[0, 1])
        last = sums[chunk][1]

    def pair_stage(chunk):
        nonlocal last
        keep, send = sums[chunk]
        last = sums[chunk] = add(keep, after(lax.ppermute(send, "ctx", pair), last))

    def output_stage(chunk):
        outs[chunk] = [
            lax.ppermute(sums[chunk][place], "ctx", ring_pairs(layers, -offset))
            if offset
            else sums[chunk][place]
            for place, offset in enumerate(offsets)
        ]

    near = [offset for offset in offsets if abs(offset) == 1]
    far = [offset for offset in offsets if abs(offset) > 1]
    bits = [1 << i for i in range(blocks.bit_length() - 1)]
    for turn in range(chunks + len(bits) + 4):
        done = []
        if 1 <= turn <= chunks:
            for offset in near:
                ring_stage(turn - 1, offset)
            done += [gathered[turn - 1][0]]
        if 2 <= turn <= chunks + 1:
            for offset in far:
                ring_stage(turn - 2, offset)
            done += [gathered[turn - 2][offset] for offset in near]
        if turn < chunks:
            attention_stage(turn, *done, *(others[-1:] if turn == 2 else ()))
        stage = turn - 2
        if 0 <= stage < chunks:
            projection_stage(stage)
        for bit in bits:
            if 0 <= stage < chunks:
                head_stage(stage, bit)
            stage -= 1
        if 0 <= stage < chunks:
            pair_stage(stage)
            output_stage(stage)
    return assemble(scalars_keep, outs, offsets, z)


def solution(mesh):
    in_specs = (
        P("ctx", "head"),
        P("ctx", "head"),
        P("ctx", None),
        P("ctx", None),
        P("head", None, None),
        P("head", None, None),
        P("head", "ctx"),
        P(),
    )
    return jax.shard_map(
        functools.partial(per_device, mesh.shape["ctx"], mesh.shape["head"]),
        mesh=mesh,
        in_specs=in_specs,
        out_specs=P(("ctx", "head"), None),
        check_vma=False,
    )
```

```python
import functools

import jax
import jax.numpy as jnp
from jax import lax
from jax.experimental import pallas as pl
from jax.experimental.pallas import tpu as pltpu
from jax.sharding import PartitionSpec as P

LATENT = 512
ROPE = 64
NOPE = 128
VDIM = 128
GROUP = 128
PAIR = 2
STEP_ROWS = 16
PAD = 128
VMEM = 24 * 1024 * 1024
SMALL_VMEM = 24 * 1024 * 1024
TINY_VMEM = 1024 * 1024
SEND_COST, KEEP_COST = 0.001, 4.0
PAUSE = 10**10
LIGHT = pl.CostEstimate(flops=1, bytes_accessed=1, transcendentals=0)


def ring_offsets(layers):
    offsets = [0]
    for step in range(1, layers // 2 + 1):
        offsets.append(step)
        if step < layers - step:
            offsets.append(-step)
    return offsets


def ring_pairs(layers, shift):
    return [
        (z * PAIR + y, (z + shift) % layers * PAIR + y) for z in range(layers) for y in range(PAIR)
    ]


def swap_pairs(size, bit):
    return [(i, i ^ bit) for i in range(size)]


def ring_gather(block, layers):
    blocks = {0: block}
    for offset in ring_offsets(layers)[1:]:
        step = 1 if offset > 0 else -1
        blocks[offset] = lax.ppermute(blocks[offset - step], "ctx", ring_pairs(layers, step))
    return [blocks[offset] for offset in ring_offsets(layers)]


def bit_reversed(index, size):
    out = 0
    while size > 1:
        out, index, size = out * 2 + index % 2, index // 2, size // 2
    return out


def prepare_kernel(offsets, scalars, order, latent_ref, rope_ref, packed_ref, key_pos_ref, query_pos_ref):
    me, y, z = scalars[1], scalars[2], scalars[3]
    block_rows = packed_ref.shape[0]
    chunks, rows, lanes = query_pos_ref.shape
    tok_rows = latent_ref.shape[0]
    layers, half = len(offsets), key_pos_ref.shape[1] // (PAIR * block_rows)
    first = pl.multiple_of(me * block_rows, block_rows)
    packed_ref[:, :LATENT] = latent_ref[pl.ds(first, block_rows), :]
    packed_ref[:, LATENT:] = jnp.concatenate(
        [rope_ref[pl.ds(first, block_rows), :], jnp.zeros((block_rows, PAD - ROPE), jnp.bfloat16)], 1
    )

    def position(row):
        group, out = row // GROUP, jnp.zeros_like(row)
        for g in range(order.shape[0]):
            out = jnp.where(group == g, order[g], out)
        return out * GROUP + row % GROUP

    shape = key_pos_ref.shape
    piece = lax.broadcasted_iota(jnp.int32, shape, 0)
    lane = lax.broadcasted_iota(jnp.int32, shape, 1)
    offset = jnp.zeros(shape, jnp.int32)
    for place, o in enumerate(offsets):
        offset = jnp.where(piece // 2 == place, o, offset)
    block = lane // (PAIR * block_rows)
    head = bit_reversed(block, half) * 2 + piece % 2 if half > 1 else piece % 2
    ctx = (z - offset + layers) % layers * PAIR + (y ^ (lane // block_rows % PAIR))
    key_pos_ref[...] = position(ctx * tok_rows + (head ^ me) * block_rows + lane % block_rows)

    shape = (rows, lanes)
    row = lax.broadcasted_iota(jnp.int32, shape, 0)
    base = (z * PAIR + y) * tok_rows + (row // STEP_ROWS ^ me) * block_rows + row % STEP_ROWS
    for chunk in range(chunks):
        query_pos_ref[chunk] = position(base + chunk * STEP_ROWS)


def prepare(scalars, order, latent, rope, blocks, offsets):
    tok_rows = latent.shape[0]
    block_rows = tok_rows // blocks
    chunks = block_rows // STEP_ROWS
    pieces, keys = 2 * len(offsets), PAIR * block_rows * blocks // 2
    vmem, smem = pl.BlockSpec(memory_space=pltpu.VMEM), pl.BlockSpec(memory_space=pltpu.SMEM)
    return pl.pallas_call(
        functools.partial(prepare_kernel, offsets),
        in_specs=[smem, smem, vmem, vmem],
        out_specs=[vmem, vmem, vmem],
        out_shape=[
            jax.ShapeDtypeStruct((block_rows, LATENT + PAD), jnp.bfloat16),
            jax.ShapeDtypeStruct((pieces, keys), jnp.int32),
            jax.ShapeDtypeStruct((chunks, blocks * STEP_ROWS, 128), jnp.int32),
        ],
        compiler_params=pltpu.CompilerParams(vmem_limit_bytes=4 * TINY_VMEM),
        cost_estimate=LIGHT,
        name="prepare",
    )(scalars, order, latent, rope)


def absorb_kernel(scalars, nope_ref, rope_ref, key_up_ref, query_ref, rotary_ref):
    chunks, heads, rows, _ = query_ref.shape
    blocks = rows // STEP_ROWS
    me = scalars[1]
    for head in range(heads):
        nope = jnp.concatenate(
            [
                nope_ref[b ^ me, c, :, head * NOPE : (head + 1) * NOPE]
                for c in range(chunks)
                for b in range(blocks)
            ],
            0,
        )
        absorbed = jnp.dot(nope, key_up_ref[head], preferred_element_type=jnp.float32)
        absorbed = absorbed.astype(jnp.bfloat16)
        for c in range(chunks):
            query_ref[c, head] = absorbed[c * rows : (c + 1) * rows]
            rotary_ref[c, head] = jnp.concatenate(
                [rope_ref[b ^ me, c, :, head * ROPE : (head + 1) * ROPE] for b in range(blocks)], 0
            )


def absorb(scalars, nope, rope, key_up):
    blocks, chunks, step_rows, _ = nope.shape
    heads, rows = key_up.shape[0], blocks * step_rows
    group = min(4, heads)
    spec = pl.BlockSpec
    return pl.pallas_call(
        absorb_kernel,
        grid_spec=pltpu.PrefetchScalarGridSpec(
            num_scalar_prefetch=1,
            grid=(heads // group,),
            in_specs=[
                spec((blocks, chunks, step_rows, group * NOPE), lambda i, s: (0, 0, 0, i)),
                spec((blocks, chunks, step_rows, group * ROPE), lambda i, s: (0, 0, 0, i)),
                spec((group, NOPE, LATENT), lambda i, s: (i, 0, 0)),
            ],
            out_specs=[
                spec((chunks, group, rows, LATENT), lambda i, s: (0, i, 0, 0)),
                spec((chunks, group, rows, ROPE), lambda i, s: (0, i, 0, 0)),
            ],
        ),
        out_shape=[
            jax.ShapeDtypeStruct((chunks, heads, rows, LATENT), jnp.bfloat16),
            jax.ShapeDtypeStruct((chunks, heads, rows, ROPE), jnp.bfloat16),
        ],
        compiler_params=pltpu.CompilerParams(vmem_limit_bytes=SMALL_VMEM),
        cost_estimate=LIGHT,
        name="absorb",
    )(scalars, nope, rope, key_up)


def attention_kernel(scalars, query_ref, rotary_ref, value_up_ref, query_pos_ref, key_pos_ref, *refs):
    piece_refs, out_ref = refs[:-1], refs[-1]
    heads, rows = query_ref.shape[1], query_ref.shape[2]
    scale = (NOPE + ROPE) ** (-0.5)
    query = query_ref[...].reshape(heads * rows, LATENT)
    rotary = rotary_ref[...].reshape(heads * rows, ROPE)
    query_pos = jnp.concatenate([query_pos_ref[0, :, :1]] * heads, 0)
    contract = (((1,), (1,)), ((), ()))
    steps = len(piece_refs) // 2

    def latent(step):
        return jnp.concatenate([ref[:, :LATENT] for ref in piece_refs[2 * step : 2 * step + 2]], 0)

    def products(step):
        keys = jnp.concatenate(
            [ref[:, LATENT : LATENT + ROPE] for ref in piece_refs[2 * step : 2 * step + 2]], 0
        )
        out = lax.dot_general(query, latent(step), contract, preferred_element_type=jnp.float32)
        return out + lax.dot_general(rotary, keys, contract, preferred_element_type=jnp.float32)

    top = jnp.full((heads * rows, 1), -1e30, jnp.float32)
    total = jnp.zeros((heads * rows, 1), jnp.float32)
    mixed = jnp.zeros((heads * rows, LATENT), jnp.float32)
    scores = products(0)
    for step in range(steps):
        later = products(step + 1) if step + 1 < steps else None
        key_pos = jnp.concatenate([key_pos_ref[2 * step + i : 2 * step + i + 1] for i in range(2)], 1)
        scores = jnp.where(key_pos <= query_pos, scores, -jnp.inf)
        new_top = jnp.maximum(top, jnp.max(scores, axis=1, keepdims=True))
        fade = jnp.exp((top - new_top) * scale)
        weights = jnp.exp((scores - new_top) * scale)
        total = total * fade + jnp.sum(weights, axis=1, keepdims=True)
        mixed = mixed * fade + jnp.dot(
            weights.astype(jnp.bfloat16), latent(step), preferred_element_type=jnp.float32
        )
        top, scores = new_top, later
    mixed = (mixed / total).astype(jnp.bfloat16)
    for head in range(heads):
        out_ref[:, head * VDIM : (head + 1) * VDIM] = jnp.dot(
            mixed[head * rows : (head + 1) * rows],
            value_up_ref[head],
            preferred_element_type=jnp.float32,
        ).astype(jnp.bfloat16)


def attend(scalars, query, rotary, value_up, query_pos, key_pos, pieces, chunk, cost):
    _, heads, rows, _ = query.shape
    heads //= PAIR
    keys = key_pos.size
    spec = pl.BlockSpec
    return pl.pallas_call(
        attention_kernel,
        grid_spec=pltpu.PrefetchScalarGridSpec(
            num_scalar_prefetch=1,
            grid=(1,),
            in_specs=[
                spec((1, heads, rows, LATENT), lambda i, s: (chunk, s[0], 0, 0)),
                spec((1, heads, rows, ROPE), lambda i, s: (chunk, s[0], 0, 0)),
                spec((heads, LATENT, VDIM), lambda i, s: (s[0], 0, 0)),
                spec((1, rows, 128), lambda i, s: (chunk, 0, 0)),
                spec(key_pos.shape, lambda i, s: (0, 0)),
            ]
            + [spec(piece.shape, lambda i, s: (0, 0)) for piece in pieces],
            out_specs=spec((rows, heads * VDIM), lambda i, s: (0, 0)),
        ),
        out_shape=jax.ShapeDtypeStruct((rows, heads * VDIM), jnp.bfloat16),
        compiler_params=pltpu.CompilerParams(vmem_limit_bytes=VMEM),
        cost_estimate=pl.CostEstimate(
            flops=int(cost * 2 * heads * rows * keys * (2 * LATENT + 256)),
            bytes_accessed=1,
            transcendentals=0,
        ),
        name="attention",
    )(scalars, query, rotary, value_up, query_pos, key_pos, *pieces)


def projection_kernel(count, layers, blocks, scalars, *refs):
    pieces, (mine_ref, *other_refs), (keep_ref, send_ref) = refs[:count], refs[count:-2], refs[-2:]
    left = jnp.concatenate([piece[...] for piece in pieces], 0)

    def product(*right_refs):
        right = jnp.concatenate([ref[...] for ref in right_refs], 0)
        out = jnp.dot(left, right, preferred_element_type=jnp.float32).astype(jnp.bfloat16)
        for index in range(count):
            rows = slice(index // layers * STEP_ROWS, (index // layers + 1) * STEP_ROWS)
            for y in range(PAIR):
                for block in range(blocks):
                    first = ((index * PAIR + y) * blocks + block) * STEP_ROWS
                    place = bit_reversed(block, blocks)
                    ref = keep_ref if place < blocks // 2 else send_ref
                    ref[place % (blocks // 2), y, index % layers, 0, rows] = out[first : first + STEP_ROWS]

    @pl.when(pl.program_id(0) == 0)
    def _():
        product(mine_ref)

    @pl.when(pl.program_id(0) == 1)
    def _():
        product(*other_refs)


def project(scalars, pieces, mine, others, blocks, layers, cost):
    count = len(pieces)
    step_rows = count // layers * STEP_ROWS
    depth, columns = mine.shape
    rows = pieces[0].shape[0]
    spec = pl.BlockSpec
    shape = (blocks // 2, PAIR, layers)
    out_spec = spec((*shape, 1, step_rows, columns), lambda i, s: (0, 0, 0, s[2] ^ i, 0, 0))
    out_shape = jax.ShapeDtypeStruct((*shape, PAIR, step_rows, columns), jnp.bfloat16)
    return pl.pallas_call(
        functools.partial(projection_kernel, count, layers, blocks),
        grid_spec=pltpu.PrefetchScalarGridSpec(
            num_scalar_prefetch=1,
            grid=(PAIR,),
            in_specs=[spec((rows, depth), lambda i, s: (0, 0))] * count
            + [spec(right.shape, lambda i, s: (0, 0)) for right in (mine, *others)],
            out_specs=[out_spec, out_spec],
        ),
        out_shape=[out_shape, out_shape],
        compiler_params=pltpu.CompilerParams(vmem_limit_bytes=SMALL_VMEM),
        cost_estimate=pl.CostEstimate(
            flops=int(cost * 2 * count * rows * depth * columns * PAIR),
            bytes_accessed=1,
            transcendentals=0,
        ),
        name="projection",
    )(scalars, *pieces, mine, *others)


def add(a, b):
    return (a.astype(jnp.float32) + b.astype(jnp.float32)).astype(jnp.bfloat16)


def pause_kernel(clock_ref, out_ref):
    del clock_ref, out_ref


def pause(clock):
    anywhere = pl.BlockSpec(memory_space=pl.ANY)
    return pl.pallas_call(
        pause_kernel,
        in_specs=[anywhere],
        out_specs=anywhere,
        out_shape=jax.ShapeDtypeStruct(clock.shape, clock.dtype),
        input_output_aliases={0: 0},
        compiler_params=pltpu.CompilerParams(vmem_limit_bytes=TINY_VMEM),
        cost_estimate=pl.CostEstimate(flops=PAUSE, bytes_accessed=1, transcendentals=0),
        name="pause",
    )(clock)


def after(value, *others):
    return lax.optimization_barrier((value, others))[0]


def assemble_kernel(offsets, scalars, clock, *refs):
    del clock
    refs, out_ref = refs[:-1], refs[-1]
    layers = len(offsets)
    z, first = scalars[3], 0
    for start in range(0, len(refs), layers):
        _, rows, columns = refs[start].shape
        for offset, ref in zip(offsets, refs[start : start + layers]):
            layer = (z + offset + layers) % layers
            for y in range(PAIR):
                column = pl.multiple_of((layer * PAIR + y) * columns, columns)
                out_ref[first : first + rows, pl.ds(column, columns)] = ref[y]
        first += rows


def assemble(scalars, outs, offsets, z, clock):
    layers = len(offsets)
    rows, columns = sum(blocks[0].shape[1] for blocks in outs), outs[0][0].shape[2]
    if columns % 128:
        parts = []
        for blocks in outs:
            arrived = dict(zip([offset % layers for offset in offsets], blocks))
            row = jnp.stack([arrived[offset] for offset in range(layers)], 0)
            row = jnp.transpose(jnp.roll(row, z, axis=0), (2, 0, 1, 3))
            parts.append(row.reshape(row.shape[0], -1))
        return jnp.concatenate(parts, 0)
    vmem, smem = pl.BlockSpec(memory_space=pltpu.VMEM), pl.BlockSpec(memory_space=pltpu.SMEM)
    flat = [block for blocks in outs for block in blocks]
    return pl.pallas_call(
        functools.partial(assemble_kernel, offsets),
        in_specs=[smem, pl.BlockSpec(memory_space=pl.ANY)] + [vmem] * len(flat),
        out_specs=vmem,
        out_shape=jax.ShapeDtypeStruct((rows, layers * PAIR * columns), flat[0].dtype),
        compiler_params=pltpu.CompilerParams(vmem_limit_bytes=8 * TINY_VMEM),
        cost_estimate=LIGHT,
        name="assemble",
    )(scalars, clock, *flat)


def per_device(
    devices, blocks, query_nope, query_rope, latent_cache, key_rope, key_up, value_up, out_proj,
    group_order,
):
    layers = devices // PAIR
    offsets = ring_offsets(layers)
    chunks = query_nope.shape[0] // blocks // STEP_ROWS
    depth = out_proj.shape[0] // PAIR
    ctx, me = lax.axis_index("ctx"), lax.axis_index("head")
    z, y = ctx // PAIR, ctx % PAIR
    pair = swap_pairs(devices, 1)
    scalars_keep = jnp.stack([y, me, y, z]).astype(jnp.int32)
    scalars_send = jnp.stack([1 - y, me, y, z]).astype(jnp.int32)

    nope = query_nope.reshape(blocks, chunks, STEP_ROWS, -1)
    rope = query_rope.reshape(blocks, chunks, STEP_ROWS, -1)

    packed, key_pos, query_pos = prepare(
        scalars_keep, group_order, latent_cache, key_rope, blocks, offsets
    )
    packed = jnp.concatenate([packed, lax.ppermute(packed, "ctx", pair)], 0)
    clock = pause(after(jnp.zeros((8, 128), jnp.int32), packed))
    mine = lax.dynamic_slice_in_dim(out_proj, y * depth, depth, 0)
    other = lax.dynamic_slice_in_dim(out_proj, (1 - y) * depth, depth, 0)
    query, rotary = absorb(after(scalars_keep, clock), nope, rope, key_up)
    cuts = [0, depth * 3 // 8, depth * 6 // 8, depth]
    others = []
    for first, end in zip(cuts[:-1], cuts[1:]):
        if others:
            other = after(other, others[-1])
        others.append(lax.ppermute(after(other[first:end], packed), "ctx", pair))
    pieces = ring_gather(packed, layers)
    pieces[1] = after(pieces[1], query, mine)
    keys = []
    for piece in pieces:
        bit = blocks // 2
        while bit > 1:
            piece = jnp.concatenate(
                [piece, lax.ppermute(piece, "head", swap_pairs(blocks, bit))], 0
            )
            bit //= 2
        keys += [piece, lax.ppermute(piece, "head", swap_pairs(blocks, 1))]

    last = others[1]
    swapped, kept, gathered, sums, outs = {}, {}, {}, {}, {}
    awaited = []
    near = [offset for offset in offsets if abs(offset) == 1]
    far = [offset for offset in offsets if abs(offset) > 1]
    bits = [1 << i for i in range(blocks.bit_length() - 1)]

    def in_order(value, *others):
        others = [last, *others, *awaited]
        awaited.clear()
        return after(value, *others)

    def attention_stage(chunk, scalars, cost, *arrived):
        nonlocal last
        last = attend(
            scalars, in_order(query, *arrived), rotary, value_up, query_pos, key_pos, keys, chunk,
            cost,
        )
        return last

    def ring_stage(chunk, offset):
        held = gathered[chunk]
        step = 1 if offset > 0 else -1
        held[offset] = lax.ppermute(held[offset - step], "ctx", ring_pairs(layers, step))

    def projection_stage(group):
        nonlocal last
        pieces = [gathered[chunk][offset] for chunk in groups[group] for offset in offsets]
        pieces[0] = in_order(pieces[0])
        cost = SEND_COST
        sums[group] = project(scalars_keep, pieces, mine, others, blocks, layers, cost)
        last = sums[group][0]

    def head_stage(group, bit):
        nonlocal last
        keep, send = sums[group]
        got = in_order(lax.ppermute(send, "head", swap_pairs(blocks, bit)))
        left = keep.shape[0] // 2
        if left:
            sums[group] = add(keep[:left], got[:left]), add(keep[left:], got[left:])
        else:
            sums[group] = add(keep[0, 0], got[0, 0]), add(keep[0, 1], got[0, 1])
        last = sums[group][1]

    def pair_stage(group):
        nonlocal last
        keep, send = sums[group]
        last = sums[group] = add(keep, in_order(lax.ppermute(send, "ctx", pair)))
        outs[group] = [
            lax.ppermute(last[place], "ctx", ring_pairs(layers, -offset)) if offset else last[place]
            for place, offset in enumerate(offsets)
        ]

    def send_half(chunk):
        arrived = [gathered[chunk - 1][0]] if chunk else []
        arrived += [gathered[chunk - 2][offset] for offset in far] if chunk > 1 else []
        sent = attention_stage(chunk, scalars_send, SEND_COST, *arrived)
        swapped[chunk] = lax.ppermute(sent, "ctx", pair)

    def keep_half(chunk):
        arrived = [gathered[chunk - 1][offset] for offset in near] if chunk else []
        arrived += others[-1:] if chunk == 1 else []
        kept[chunk] = attention_stage(chunk, scalars_keep, KEEP_COST, *arrived)
        gathered[chunk] = {0: jnp.concatenate([kept[chunk], swapped[chunk]], 0)}
        for offset in near if chunk == released else near + far:
            ring_stage(chunk, offset)

    def release(chunk):
        for offset in far:
            if abs(offset) == 2:
                held = gathered[chunk]
                held[offset // 2] = after(held[offset // 2], clock)
            ring_stage(chunk, offset)

    def pause_stage():
        nonlocal last, clock
        last = clock = pause(in_order(clock))

    if chunks == 4:
        groups = [[0, 1], [2], [3]]
        released = 3
        plan = [
            (send_half, 0), (keep_half, 0), (pause_stage,),
            (send_half, 1), (keep_half, 1), (pause_stage,),
            (send_half, 2), (keep_half, 2), (pause_stage,),
            (send_half, 3), (projection_stage, 0), (keep_half, 3), (pause_stage,),
            (head_stage, 0, 1), (pause_stage,),
            (projection_stage, 1), (pause_stage,),
            (head_stage, 1, 1), (release, 3), (pause_stage,),
            (projection_stage, 2), (pause_stage,),
            (head_stage, 0, 2), (pause_stage,),
            (head_stage, 2, 1), (pause_stage,),
            (head_stage, 1, 2), (pause_stage,),
            (pair_stage, 0), (pause_stage,),
            (pair_stage, 1), (pause_stage,),
            (head_stage, 2, 2), (pause_stage,),
            (pair_stage, 2),
        ]
    else:
        groups = [[chunk] for chunk in range(chunks)]
        released = None
        plan = []
        for chunk in range(chunks):
            plan += [(send_half, chunk), (keep_half, chunk), (projection_stage, chunk)]
            plan += [(head_stage, chunk, bit) for bit in bits] + [(pair_stage, chunk)]
    for stage, *where in plan:
        stage(*where)
    return assemble(scalars_keep, [outs[g] for g in range(len(groups))], offsets, z, clock)


def solution(mesh):
    in_specs = (
        P("ctx", "head"),
        P("ctx", "head"),
        P("ctx", None),
        P("ctx", None),
        P("head", None, None),
        P("head", None, None),
        P("head", "ctx"),
        P(),
    )
    return jax.shard_map(
        functools.partial(per_device, mesh.shape["ctx"], mesh.shape["head"]),
        mesh=mesh,
        in_specs=in_specs,
        out_specs=P(("ctx", "head"), None),
        check_vma=False,
    )
```
